256 devices in a mesh: wide: 32 (over y, x, core), narrow: 8 (over z).
Axes of the slice: x: 4, y: 4, z: 8, core: 2. Of those that a mesh axis runs over, the one named last changes fastest.
Arguments:
- amplitudes: bfloat16 [4096, 10240], P(('narrow', 'wide')), may hold values from -6 to 6
- integrals: bfloat16 [10240, 20480], P('narrow', 'wide'), may hold values from -0.15625 to 0.15625
- other_terms: bfloat16 [4096, 20480], P('narrow', 'wide'), may hold values from -6 to 6
- occ_energy: float32 [64], replicated, may hold values from -2 to -0.5
- virt_energy: float32 [640], replicated, may hold values from 0.2 to 3
- occ_irrep: int32 [64], replicated, may hold values from 0 to 7
- virt_irrep: int32 [640], replicated, may hold values from 0 to 7
- tiles_e: int32 [1], replicated, may hold values from 0 to 39
- tiles_a: int32 [2], replicated, may hold values from 0 to 39
Outputs:
- new_amplitudes: float32 [4096, 20480], P('narrow', 'wide')
The draws below stay inside these ranges and needn't reach their ends.
All inputs are finite; a program needn't handle non-finite values.
Results may differ from the reference program's by a relative error of at most 0.0003.
Values may be sent and summed in bfloat16 or wider, within the bound.
No kernel may reach another device: no remote copies, remote signals or barrier semaphores. Data moves between devices by JAX's collectives and lax.ppermute only.
A program may use at most 128 MiB of HBM per device.

```python
import jax
import jax.numpy as jnp

NVIR = 640
NOCC = 64
TILE = 16
E_TILES = 1
A_TILES = 2
OCC_PAIRS = 4096
EF_PAIRS = 10240
AB_PAIRS = 20480


def set_ends(entries, own_key, least, top_value):
    longest = entries.shape.index(max(entries.shape))
    spots = []
    for shift in (0, 1):
        where = [jax.random.randint(jax.random.fold_in(own_key, axis), (), 0, length) for axis, length in enumerate(entries.shape)]
        where[longest] = (where[longest] + shift) % entries.shape[longest]
        spots.append(tuple(where))
    return entries.at[spots[0]].set(least).at[spots[1]].set(top_value)


def shard_levels(own_key, dims, shards, least, top_value):
    factor_of, own = 1.0, jax.random.fold_in(own_key, 6)
    for position, parts in shards:
        draws = jnp.exp(jax.random.uniform(jax.random.fold_in(own, position), (parts,), jnp.float32, least / len(shards), top_value / len(shards)))
        factor_of = factor_of * jnp.repeat(draws, dims[position] // parts).reshape([-1 if axis == position else 1 for axis in range(len(dims))])
    return factor_of


def noise(key, shape, scale, limit, split=(), held_as=jnp.bfloat16):
    entries = jax.random.normal(key, shape, jnp.float32) * scale
    if len(split) > 0:
        entries = shard_levels(key, shape, split, -0.22, 0.18) * entries
    return jnp.clip(entries, min=-limit, max=limit).astype(held_as)


def setup_inputs(seed: int = 0) -> dict:
    seeds = jax.random.split(jax.random.key(seed), 10)
    return {
        "amplitudes": noise(seeds[0], (OCC_PAIRS, EF_PAIRS), 1.0, 6.0, ((0, 256),)),
        "integrals": noise(seeds[1], (EF_PAIRS, AB_PAIRS), (EF_PAIRS // 8) ** -0.5, 0.15625, ((0, 8), (1, 32))),
        "other_terms": noise(seeds[2], (OCC_PAIRS, AB_PAIRS), 1.0, 6.0, ((0, 8), (1, 32))),
        "occ_energy": jnp.clip(jax.random.uniform(seeds[3], (NOCC,), jnp.float32, -2.0, -0.5), -2.0, -0.5),
        "virt_energy": jnp.clip(jax.random.uniform(seeds[4], (NVIR,), jnp.float32, 0.2, 3.0), 0.2, 3.0),
        "occ_irrep": set_ends(jax.random.randint(seeds[5], (NOCC,), 0, 8), jax.random.fold_in(seeds[5], 1), 0, 7).astype(jnp.int32),
        "virt_irrep": set_ends(jax.random.randint(seeds[6], (NVIR,), 0, 8), jax.random.fold_in(seeds[6], 1), 0, 7).astype(jnp.int32),
        "tiles_e": jax.random.randint(seeds[7], (E_TILES,), 0, NVIR // TILE).astype(jnp.int32),
        "tiles_a": jax.random.randint(seeds[8], (A_TILES,), 0, NVIR // TILE).astype(jnp.int32),
    }


def reference(amplitudes, integrals, other_terms, occ_energy, virt_energy, occ_irrep, virt_irrep, tiles_e, tiles_a):
    offsets = jnp.arange(TILE, dtype=jnp.int32)
    e_index = (tiles_e[:, None] * TILE + offsets[None, :]).reshape(-1)
    a_index = (tiles_a[:, None] * TILE + offsets[None, :]).reshape(-1)
    ef_sym = jnp.bitwise_xor(virt_irrep[e_index][:, None], virt_irrep[None, :]).reshape(-1)
    ab_sym = jnp.bitwise_xor(virt_irrep[a_index][:, None], virt_irrep[None, :]).reshape(-1)
    ab_energy = (virt_energy[a_index][:, None] + virt_energy[None, :]).reshape(-1)
    ij_sym = jnp.bitwise_xor(occ_irrep[:, None], occ_irrep[None, :]).reshape(-1)
    ij_energy = (occ_energy[:, None] + occ_energy[None, :]).reshape(-1)
    width = TILE * NVIR
    results = []
    for a_block in range(A_TILES):
        first_col = a_block * width
        col_sym = ab_sym[first_col:first_col + width]
        col_energy = ab_energy[first_col:first_col + width]
        masked = jnp.where(ef_sym[:, None] == col_sym[None, :], integrals[:, first_col:first_col + width], jnp.zeros((), integrals.dtype))
        ladder = jnp.dot(amplitudes, masked, preferred_element_type=jnp.float32)
        summed = ladder + other_terms[:, first_col:first_col + width].astype(jnp.float32)
        denom = ij_energy[:, None] - col_energy[None, :]
        results.append(jnp.where(ij_sym[:, None] == col_sym[None, :], summed / denom, jnp.zeros((), jnp.float32)))
    return jnp.concatenate(results, axis=1)
```

```python
import jax
import jax.numpy as jnp
from jax import lax
from jax.experimental import pallas as pl
from jax.experimental.pallas import tpu as pltpu
from jax.sharding import PartitionSpec as P

TILE = 16
NVIR = 640
NOCC = 64
IRREPS = 8
CAP = 112
PITCH = 128
E_LOCAL = 2
VMEM_LIMIT = 56 * 1024 * 1024

SMEM = pl.BlockSpec(memory_space=pltpu.SMEM)
VMEM = pl.BlockSpec(memory_space=pltpu.VMEM)


def selector(irrep_row):
    group = lax.broadcasted_iota(jnp.int32, (IRREPS, NVIR), 0)
    member = irrep_row == group
    earlier = lax.broadcasted_iota(jnp.int32, (NVIR, NVIR), 0) < lax.broadcasted_iota(
        jnp.int32, (NVIR, NVIR), 1
    )
    before = jnp.dot(
        member.astype(jnp.bfloat16),
        earlier.astype(jnp.bfloat16),
        preferred_element_type=jnp.float32,
    )
    rank = jnp.sum(jnp.where(member, before, 0.0), axis=0, keepdims=True).astype(jnp.int32)
    place = jnp.where(rank < CAP, irrep_row * PITCH + rank, -1)
    slots = lax.broadcasted_iota(jnp.int32, (IRREPS * PITCH, NVIR), 0)
    return (slots == place).astype(jnp.bfloat16)


def pack_amplitudes(irrep_s, occ_s, tiles_e_s, irrep_row, rows_ref, out_ref, stacked):
    wide, narrow = lax.axis_index("wide"), lax.axis_index("narrow")
    e_count = rows_ref.shape[1] // NVIR
    height = rows_ref.shape[0]
    for e in range(e_count):
        stacked[e * height:(e + 1) * height, :] = rows_ref[:, e * NVIR:(e + 1) * NVIR]
    picked = lax.dot_general(
        stacked[...],
        selector(irrep_row[...]),
        (((1,), (1,)), ((), ())),
        preferred_element_type=jnp.float32,
    )
    first = (narrow * 32 + wide) * height
    line = lax.broadcasted_iota(jnp.int32, (height, PITCH), 0)
    occ = jnp.zeros((height, PITCH), jnp.int32)
    for row in range(height):
        pair = first + row
        sym = occ_s[pair // NOCC] ^ occ_s[pair % NOCC]
        occ = jnp.where(line == row, sym, occ)
    for e in range(e_count):
        wanted = occ ^ irrep_s[tiles_e_s[0] * TILE + e]
        block = jnp.zeros((height, PITCH), jnp.float32)
        for g in range(IRREPS):
            block = jnp.where(
                wanted == g,
                picked[e * height:(e + 1) * height, g * PITCH:(g + 1) * PITCH],
                block,
            )
        out_ref[:, e * PITCH:(e + 1) * PITCH] = block.astype(out_ref.dtype)


def pack_integrals(irrep_s, tiles_e_s, tiles_a_s, irrep_row, panel_ref, out_ref):
    wide, narrow = lax.axis_index("wide"), lax.axis_index("narrow")
    a = tiles_a_s[wide // TILE] * TILE + wide % TILE
    picks = selector(irrep_row[...])
    for local in range(E_LOCAL):
        e = tiles_e_s[0] * TILE + narrow * E_LOCAL + local
        wanted = irrep_row[...] ^ (irrep_s[a] ^ irrep_s[e])
        panel = panel_ref[local * NVIR:(local + 1) * NVIR, :]
        block = jnp.zeros((CAP, NVIR), jnp.float32)
        for g in range(IRREPS):
            picked = jnp.dot(
                picks[g * PITCH:g * PITCH + CAP, :], panel, preferred_element_type=jnp.float32
            )
            block = jnp.where(wanted == g, picked, block)
        out_ref[local * CAP:(local + 1) * CAP, :] = block.astype(out_ref.dtype)


def as_column(row):
    width = row.shape[1]
    across = lax.broadcasted_iota(jnp.int32, (width, width), 1)
    down = lax.broadcasted_iota(jnp.int32, (width, width), 0)
    return jnp.sum(jnp.where(across == down, row, jnp.zeros_like(row)), axis=1, keepdims=True)


def contract(
    irrep_s, energy_s, occ_irrep_s, occ_energy_s, tiles_a_s,
    irrep_row, energy_row, occ_irrep_row, occ_energy_row,
    amplitudes, panel, other, out_ref, spread,
):
    wide, narrow = lax.axis_index("wide"), lax.axis_index("narrow")
    e_count = amplitudes.shape[1] // PITCH
    for e in range(e_count):
        spread[e * PITCH:e * PITCH + CAP, :] = panel[e * CAP:(e + 1) * CAP, :]
        spread[e * PITCH + CAP:(e + 1) * PITCH, :] = jnp.zeros(
            (PITCH - CAP, NVIR), spread.dtype
        )
    a = tiles_a_s[wide // TILE] * TILE + wide % TILE
    col_sym = irrep_row[...] ^ irrep_s[a]
    col_energy = energy_s[a] + energy_row[...]
    j_sym = as_column(occ_irrep_row[...])
    j_energy = as_column(occ_energy_row[...])
    i_count = out_ref.shape[0] // NOCC
    ladder = jnp.dot(amplitudes[...], spread[...], preferred_element_type=jnp.float32)
    for local in range(i_count):
        i = narrow * i_count + local
        rows = slice(local * NOCC, (local + 1) * NOCC)
        summed = ladder[rows, :] + other[rows, :].astype(jnp.float32)
        denom = (occ_energy_s[i] + j_energy) - col_energy
        same = (j_sym ^ occ_irrep_s[i]) == col_sym
        out_ref[rows, :] = jnp.where(same, summed / denom, 0.0)


def packed_plan(
    amplitudes, integrals, other_terms, occ_energy, virt_energy, occ_irrep, virt_irrep, tiles_e, tiles_a
):
    irrep_row = virt_irrep.reshape(1, NVIR)
    params = pltpu.CompilerParams(vmem_limit_bytes=VMEM_LIMIT)
    height, width = amplitudes.shape
    e_count = width // NVIR
    small = pl.pallas_call(
        pack_amplitudes,
        out_shape=jax.ShapeDtypeStruct((height, e_count * PITCH), amplitudes.dtype),
        in_specs=[SMEM, SMEM, SMEM, VMEM, VMEM],
        out_specs=VMEM,
        scratch_shapes=[pltpu.VMEM((e_count * height, NVIR), amplitudes.dtype)],
        compiler_params=params,
        name="pack_amplitudes",
    )(virt_irrep, occ_irrep, tiles_e, irrep_row, amplitudes)
    rows = lax.all_gather(small, "wide", axis=0, tiled=True)
    strip = pl.pallas_call(
        pack_integrals,
        out_shape=jax.ShapeDtypeStruct((E_LOCAL * CAP, NVIR), integrals.dtype),
        in_specs=[SMEM, SMEM, SMEM, VMEM, VMEM],
        out_specs=VMEM,
        compiler_params=params,
        name="pack_integrals",
    )(virt_irrep, tiles_e, tiles_a, irrep_row, integrals)
    panel = lax.all_gather(strip, "narrow", axis=0, tiled=True)
    return pl.pallas_call(
        contract,
        out_shape=jax.ShapeDtypeStruct(other_terms.shape, jnp.float32),
        in_specs=[SMEM] * 5 + [VMEM] * 7,
        out_specs=VMEM,
        scratch_shapes=[pltpu.VMEM((e_count * PITCH, NVIR), integrals.dtype)],
        compiler_params=params,
        name="contract",
    )(
        virt_irrep, virt_energy, occ_irrep, occ_energy, tiles_a,
        irrep_row, virt_energy.reshape(1, NVIR),
        occ_irrep.reshape(1, NOCC), occ_energy.reshape(1, NOCC),
        rows, panel, other_terms,
    )


def pair_labels(tiles, lookup_table):
    offsets = jnp.arange(TILE, dtype=jnp.int32)
    orbital_index = (tiles[:, None] * TILE + offsets[None, :]).reshape(-1)
    matches = orbital_index[:, None] == jnp.arange(lookup_table.shape[0], dtype=jnp.int32)[None, :]
    return jnp.sum(
        jnp.where(matches, lookup_table[None, :], jnp.zeros((), lookup_table.dtype)), axis=1
    )


def dense_plan(
    amplitudes, integrals, other_terms, occ_energy, virt_energy, occ_irrep, virt_irrep, tiles_e, tiles_a
):
    gathered = lax.all_gather(amplitudes, "wide", axis=0, tiled=True)
    ef_sym = jnp.bitwise_xor(
        pair_labels(tiles_e, virt_irrep)[:, None], virt_irrep[None, :]
    ).reshape(-1)
    ab_sym_all = jnp.bitwise_xor(
        pair_labels(tiles_a, virt_irrep)[:, None], virt_irrep[None, :]
    ).reshape(-1)
    ab_energy_all = (pair_labels(tiles_a, virt_energy)[:, None] + virt_energy[None, :]).reshape(-1)
    col_width = integrals.shape[1]
    col_first = lax.axis_index("wide") * col_width
    col_sym = lax.dynamic_slice_in_dim(ab_sym_all, col_first, col_width)
    col_energy = lax.dynamic_slice_in_dim(ab_energy_all, col_first, col_width)
    row_height = gathered.shape[0]
    row_first = lax.axis_index("narrow") * row_height
    ij_sym = lax.dynamic_slice_in_dim(
        jnp.bitwise_xor(occ_irrep[:, None], occ_irrep[None, :]).reshape(-1), row_first, row_height
    )
    ij_energy = lax.dynamic_slice_in_dim(
        (occ_energy[:, None] + occ_energy[None, :]).reshape(-1), row_first, row_height
    )
    panel_rows = lax.all_gather(integrals, "narrow", axis=0, tiled=True)
    masked = jnp.where(
        ef_sym[:, None] == col_sym[None, :], panel_rows, jnp.zeros((), panel_rows.dtype)
    )
    ladder = jnp.dot(gathered, masked, preferred_element_type=jnp.float32)
    summed = ladder + other_terms.astype(jnp.float32)
    denom = ij_energy[:, None] - col_energy[None, :]
    return jnp.where(
        ij_sym[:, None] == col_sym[None, :], summed / denom, jnp.zeros((), jnp.float32)
    )


def shards(*args):
    virt_irrep = args[6]
    held = jnp.sum(
        virt_irrep[None, :] == jnp.arange(IRREPS, dtype=jnp.int32)[:, None], axis=1, dtype=jnp.int32
    )
    return lax.cond(jnp.max(held) <= CAP, packed_plan, dense_plan, *args)


def solution(mesh):
    in_specs = (
        P(("narrow", "wide"), None),
        P("narrow", "wide"),
        P("narrow", "wide"),
        P(),
        P(),
        P(),
        P(),
        P(),
        P(),
    )
    out_specs = P("narrow", "wide")
    return jax.shard_map(shards, mesh=mesh, in_specs=in_specs, out_specs=out_specs, check_vma=False)
```

```python
import jax
import jax.numpy as jnp
from jax import lax
from jax.experimental import pallas as pl
from jax.experimental.pallas import tpu as pltpu
from jax.sharding import PartitionSpec as P

TILE = 16
NVIR = 640
NOCC = 64
IRREPS = 8
CAP = 112
PITCH = 128
E_LOCAL = 2
RING = 8
SIDE = 4
ROWS = 16
VMEM_LIMIT = 56 * 1024 * 1024

SMEM = pl.BlockSpec(memory_space=pltpu.SMEM)
VMEM = pl.BlockSpec(memory_space=pltpu.VMEM)


def pack(
    base_s, irrep_s, occ_s, tiles_e_s, tiles_a_s, irrep_row, rows_ref, panel_ref,
    first_ref, second_ref, out_ref, stacked,
):
    wide, narrow = lax.axis_index("wide"), lax.axis_index("narrow")
    e_first = tiles_e_s[0] * TILE
    irreps = irrep_row[...]

    group = lax.broadcasted_iota(jnp.int32, (IRREPS, NVIR), 0)
    member = irreps == group
    earlier = lax.broadcasted_iota(jnp.int32, (NVIR, NVIR), 0) < lax.broadcasted_iota(
        jnp.int32, (NVIR, NVIR), 1
    )
    before = jnp.dot(
        member.astype(jnp.bfloat16),
        earlier.astype(jnp.bfloat16),
        preferred_element_type=jnp.float32,
    )
    rank = jnp.sum(jnp.where(member, before, 0.0), axis=0, keepdims=True).astype(jnp.int32)
    place = rank - base_s[0]
    slots = lax.broadcasted_iota(jnp.int32, (PITCH, NVIR), 0)
    picks = ((slots == place) & (slots < CAP)).astype(jnp.bfloat16)

    a = tiles_a_s[wide // TILE] * TILE + wide % TILE
    irrep_col = jnp.transpose(jnp.broadcast_to(irreps, (PITCH, NVIR)))
    for local, strip_ref in enumerate((first_ref, second_ref)):
        wanted = irreps ^ (irrep_s[a] ^ irrep_s[e_first + narrow * E_LOCAL + local])
        for tile in range(NVIR // PITCH):
            lanes = slice(tile * PITCH, (tile + 1) * PITCH)
            kept = jnp.where(
                irrep_col == wanted[:, lanes],
                panel_ref[local * NVIR:(local + 1) * NVIR, lanes].astype(jnp.float32),
                0.0,
            ).astype(jnp.bfloat16)
            strip_ref[:, lanes] = jnp.dot(
                picks[:CAP, :], kept, preferred_element_type=jnp.float32
            ).astype(strip_ref.dtype)

    first = (narrow * 32 + wide) * ROWS
    line = lax.broadcasted_iota(jnp.int32, (ROWS, NVIR), 0)
    occ = jnp.zeros((ROWS, NVIR), jnp.int32)
    for row in range(ROWS):
        pair = first + row
        occ = jnp.where(line == row, occ_s[pair // NOCC] ^ occ_s[pair % NOCC], occ)
    kin = occ ^ irreps
    for e in range(TILE):
        stacked[e * ROWS:(e + 1) * ROWS, :] = jnp.where(
            kin == irrep_s[e_first + e],
            rows_ref[:, e * NVIR:(e + 1) * NVIR].astype(jnp.float32),
            0.0,
        ).astype(jnp.bfloat16)
    picked = lax.dot_general(
        stacked[...], picks, (((1,), (1,)), ((), ())), preferred_element_type=jnp.float32
    ).astype(out_ref.dtype)
    for e in range(TILE):
        out_ref[:, e * PITCH:(e + 1) * PITCH] = picked[e * ROWS:(e + 1) * ROWS, :]


def as_column(row):
    width = row.shape[1]
    across = lax.broadcasted_iota(jnp.int32, (width, width), 1)
    down = lax.broadcasted_iota(jnp.int32, (width, width), 0)
    return jnp.sum(jnp.where(across == down, row, jnp.zeros_like(row)), axis=1, keepdims=True)


def reach(index):
    return (0, -1, 1, 2)[index]


def contract(
    irrep_s, energy_s, occ_irrep_s, occ_energy_s, tiles_a_s,
    irrep_row, energy_row, occ_irrep_row, occ_energy_row, other, own, twin, *refs,
):
    strips, out_ref, amplitudes, panel = refs[:2 * RING], refs[-3], refs[-2], refs[-1]
    wide, narrow = lax.axis_index("wide"), lax.axis_index("narrow")
    y, x, core = wide // 8, wide // 2 % SIDE, wide % 2
    for ref, side in ((own, core), (twin, 1 - core)):
        for outer in range(SIDE):
            for inner in range(SIDE):
                dx = jnp.where(side == 0, reach(inner), reach(outer))
                dy = jnp.where(side == 0, reach(outer), reach(inner))
                place = (y + dy + SIDE) % SIDE * 8 + (x + dx + SIDE) % SIDE * 2 + side
                block = (outer * SIDE + inner) * ROWS
                amplitudes[pl.ds(pl.multiple_of(place * ROWS, ROWS), ROWS), :] = ref[
                    block:block + ROWS, :
                ]
    blank = jnp.zeros((PITCH - CAP, NVIR), panel.dtype)
    for step in range(RING):
        source = (narrow - step + RING) % RING
        for local in range(E_LOCAL):
            start = pl.multiple_of((source * E_LOCAL + local) * PITCH, PITCH)
            panel[pl.ds(start, CAP), :] = strips[step * E_LOCAL + local][...]
            panel[pl.ds(pl.multiple_of(start + CAP, 16), PITCH - CAP), :] = blank
    a = tiles_a_s[wide // TILE] * TILE + wide % TILE
    col_sym = irrep_row[...] ^ irrep_s[a]
    col_energy = energy_s[a] + energy_row[...]
    j_sym = as_column(occ_irrep_row[...])
    j_energy = as_column(occ_energy_row[...])
    i_count = out_ref.shape[0] // NOCC
    ladder = jnp.dot(amplitudes[...], panel[...], preferred_element_type=jnp.float32)
    for local in range(i_count):
        i = narrow * i_count + local
        rows = slice(local * NOCC, (local + 1) * NOCC)
        summed = ladder[rows, :] + other[rows, :].astype(jnp.float32)
        denom = (occ_energy_s[i] + j_energy) - col_energy
        same = (j_sym ^ occ_irrep_s[i]) == col_sym
        out_ref[rows, :] = jnp.where(same, summed / denom, 0.0)


def ring(shift):
    return [(i, (i + shift) % RING) for i in range(RING)]


def plane(along_x, along_y):
    pairs = []
    for i in range(32):
        y, x, core = i // 8, i // 2 % SIDE, i % 2
        dx, dy = (along_x, along_y) if core == 0 else (along_y, along_x)
        pairs.append((i, (y + dy) % SIDE * 8 + (x + dx) % SIDE * 2 + core))
    return pairs


def spread(block, steps):
    parts = [block] + [lax.ppermute(block, "wide", pairs) for pairs in steps]
    return jnp.concatenate(parts, axis=0)


def one_pass(
    base, amplitudes, integrals, other_terms,
    occ_energy, virt_energy, occ_irrep, virt_irrep, tiles_e, tiles_a,
):
    irrep_row = virt_irrep.reshape(1, NVIR)
    params = pltpu.CompilerParams(vmem_limit_bytes=VMEM_LIMIT)
    strip = jax.ShapeDtypeStruct((CAP, NVIR), integrals.dtype)
    first, second, block = pl.pallas_call(
        pack,
        out_shape=(strip, strip, jax.ShapeDtypeStruct((ROWS, TILE * PITCH), amplitudes.dtype)),
        in_specs=[SMEM] * 5 + [VMEM] * 3,
        out_specs=(VMEM,) * 3,
        scratch_shapes=[pltpu.VMEM((TILE * ROWS, NVIR), amplitudes.dtype)],
        compiler_params=params,
        name="pack",
    )(base, virt_irrep, occ_irrep, tiles_e, tiles_a, irrep_row, amplitudes, integrals)

    strips = [None] * RING
    strips[0] = [first, second]
    up, down = strips[0], strips[0]
    for step in range(1, RING // 2):
        up = [lax.ppermute(part, "narrow", ring(1)) for part in up]
        down = [lax.ppermute(part, "narrow", ring(-1)) for part in down]
        strips[step], strips[RING - step] = up, down
    strips[RING // 2] = [
        lax.ppermute(up[0], "narrow", ring(1)), lax.ppermute(down[1], "narrow", ring(-1))
    ]

    own = spread(block, [plane(1, 0), plane(-1, 0), plane(2, 0)])
    own = spread(own, [plane(0, 1), plane(0, -1), plane(0, 2)])
    twin = lax.ppermute(own, "wide", [(i, i ^ 1) for i in range(32)])

    return pl.pallas_call(
        contract,
        out_shape=jax.ShapeDtypeStruct(other_terms.shape, jnp.float32),
        in_specs=[SMEM] * 5 + [VMEM] * (7 + 2 * RING),
        out_specs=VMEM,
        scratch_shapes=[
            pltpu.VMEM((other_terms.shape[0], TILE * PITCH), amplitudes.dtype),
            pltpu.VMEM((TILE * PITCH, NVIR), integrals.dtype),
        ],
        compiler_params=params,
        name="contract",
    )(
        virt_irrep, virt_energy, occ_irrep, occ_energy, tiles_a,
        irrep_row, virt_energy.reshape(1, NVIR),
        occ_irrep.reshape(1, NOCC), occ_energy.reshape(1, NOCC),
        other_terms, own, twin, *[part for pair in strips for part in pair],
    )


def shards(amplitudes, integrals, other_terms, *tables):
    virt_irrep = tables[3]
    held = jnp.sum(
        virt_irrep[None, :] == jnp.arange(IRREPS, dtype=jnp.int32)[:, None], axis=1, dtype=jnp.int32
    )
    most = jnp.max(held)

    def more(state):
        return state[0] < most

    def add_pass(state):
        base, total = state
        part = one_pass(
            base.reshape(1), amplitudes, integrals, jnp.zeros_like(other_terms), *tables
        )
        return base + CAP, total + part

    whole = one_pass(jnp.zeros((1,), jnp.int32), amplitudes, integrals, other_terms, *tables)
    return lax.while_loop(more, add_pass, (jnp.int32(CAP), whole))[1]


def solution(mesh):
    in_specs = (
        P(("narrow", "wide"), None),
        P("narrow", "wide"),
        P("narrow", "wide"),
        P(),
        P(),
        P(),
        P(),
        P(),
        P(),
    )
    out_specs = P("narrow", "wide")
    return jax.shard_map(shards, mesh=mesh, in_specs=in_specs, out_specs=out_specs, check_vma=False)
```

```python
import jax
import jax.numpy as jnp
from jax import lax
from jax.experimental import pallas as pl
from jax.experimental.pallas import tpu as pltpu
from jax.sharding import PartitionSpec as P

TILE = 16
NVIR = 640
NOCC = 64
IRREPS = 8
CAP = 112
PITCH = 128
E_LOCAL = 2
RING = 8
SIDE = 4
ROWS = 16

SMEM = pl.BlockSpec(memory_space=pltpu.SMEM)
VMEM = pl.BlockSpec(memory_space=pltpu.VMEM)
ANY = pl.BlockSpec(memory_space=pl.ANY)
HBM = pl.BlockSpec(memory_space=pltpu.HBM)


def params(mib):
    return pltpu.CompilerParams(vmem_limit_bytes=mib * 1024 * 1024)


def pack_integrals(
    base_s, irrep_s, tiles_e_s, tiles_a_s, irrep_ref, panel_hbm,
    strip_ref, picks_ref, most_s, panel_ref, arrived,
):
    fetches = [
        pltpu.make_async_copy(
            panel_hbm.at[pl.ds(local * NVIR, NVIR), :], panel_ref.at[local], arrived.at[local]
        )
        for local in range(E_LOCAL)
    ]
    for fetch in fetches:
        fetch.start()
    wide, narrow = lax.axis_index("wide"), lax.axis_index("narrow")
    irreps = irrep_ref[...].reshape(1, NVIR)
    group = lax.broadcasted_iota(jnp.int32, (IRREPS, NVIR), 0)
    member = irreps == group
    earlier = lax.broadcasted_iota(jnp.int32, (NVIR, NVIR), 0) < lax.broadcasted_iota(
        jnp.int32, (NVIR, NVIR), 1
    )
    before = jnp.dot(
        member.astype(jnp.bfloat16),
        earlier.astype(jnp.bfloat16),
        preferred_element_type=jnp.float32,
    )
    rank = jnp.sum(jnp.where(member, before, 0.0), axis=0, keepdims=True).astype(jnp.int32)
    most_s[0] = jnp.max(rank) + 1
    slots = lax.broadcasted_iota(jnp.int32, (PITCH, NVIR), 0)
    picks = ((slots == rank - base_s[0]) & (slots < CAP)).astype(jnp.bfloat16)
    picks_ref[...] = picks

    a = tiles_a_s[wide // TILE] * TILE + wide % TILE
    labels = jnp.broadcast_to(irreps, (PITCH, NVIR)).astype(jnp.float32)
    label_col = jnp.transpose(labels).astype(jnp.bfloat16)
    for local in range(E_LOCAL):
        e = tiles_e_s[0] * TILE + narrow * E_LOCAL + local
        wanted = (irreps ^ (irrep_s[a] ^ irrep_s[e])).astype(jnp.float32).astype(jnp.bfloat16)
        fetches[local].wait()
        for tile in range(NVIR // PITCH):
            lanes = slice(tile * PITCH, (tile + 1) * PITCH)
            held = panel_ref[local, :, lanes]
            kept = jnp.where(label_col == wanted[:, lanes], held, jnp.zeros_like(held))
            strip_ref[local * CAP:(local + 1) * CAP, lanes] = jnp.dot(
                picks[:CAP, :], kept, preferred_element_type=jnp.float32
            ).astype(strip_ref.dtype)


def pack_amplitudes(irrep_s, occ_s, tiles_e_s, irrep_ref, picks_ref, rows_ref, out_ref, stacked):
    wide, narrow = lax.axis_index("wide"), lax.axis_index("narrow")
    irreps = irrep_ref[...].reshape(1, NVIR)
    first = (narrow * 32 + wide) * ROWS
    line = lax.broadcasted_iota(jnp.int32, (ROWS, NVIR), 0)
    occ = jnp.zeros((ROWS, NVIR), jnp.int32)
    for row in range(ROWS):
        pair = first + row
        occ = jnp.where(line == row, occ_s[pair // NOCC] ^ occ_s[pair % NOCC], occ)
    kin = (occ ^ irreps).astype(jnp.float32).astype(jnp.bfloat16)
    for e in range(TILE):
        held = rows_ref[:, e * NVIR:(e + 1) * NVIR]
        label = irrep_s[tiles_e_s[0] * TILE + e].astype(jnp.float32).astype(jnp.bfloat16)
        stacked[e * ROWS:(e + 1) * ROWS, :] = jnp.where(kin == label, held, jnp.zeros_like(held))
    picked = lax.dot_general(
        stacked[...], picks_ref[...], (((1,), (1,)), ((), ())), preferred_element_type=jnp.float32
    ).astype(out_ref.dtype)
    for e in range(TILE):
        out_ref[:, e * PITCH:(e + 1) * PITCH] = picked[e * ROWS:(e + 1) * ROWS, :]


def stack(parts, after=()):
    height, width = parts[0].shape

    def place(*refs):
        for index in range(len(parts)):
            refs[-1][index * height:(index + 1) * height, :] = refs[index][...]

    return pl.pallas_call(
        place,
        out_shape=jax.ShapeDtypeStruct((len(parts) * height, width), parts[0].dtype),
        in_specs=[VMEM] * len(parts) + [ANY] * len(after),
        out_specs=VMEM,
        compiler_params=params(6),
        name="stack",
    )(*parts, *after)


def as_column(row):
    width = row.shape[1]
    across = lax.broadcasted_iota(jnp.int32, (width, width), 1)
    down = lax.broadcasted_iota(jnp.int32, (width, width), 0)
    return jnp.sum(jnp.where(across == down, row, jnp.zeros_like(row)), axis=1, keepdims=True)


def reach(index):
    return (0, -1, 1, 2)[index]


def fill(panel, strips):
    blank = jnp.zeros((PITCH - CAP, NVIR), panel.dtype)
    for index, strip in enumerate(strips):
        for local in range(E_LOCAL):
            start = (index * E_LOCAL + local) * PITCH
            panel[start:start + CAP, :] = strip[local * CAP:(local + 1) * CAP, :]
            panel[start + CAP:start + PITCH, :] = blank


def columns_of(amplitudes, step):
    way = 1 - 2 * (lax.axis_index("wide") % 2)
    source = (lax.axis_index("narrow") - way * step + RING) % RING
    start = pl.multiple_of(source * E_LOCAL * PITCH, E_LOCAL * PITCH)
    return amplitudes[:, pl.ds(start, E_LOCAL * PITCH)]


def contract_early(steps, late_steps, other, own, twin, *refs):
    strips, (sum_ref, late_ref, amplitudes, ordered, panel) = refs[:-5], refs[-5:]
    wide = lax.axis_index("wide")
    y, x, core = wide // 8, wide // 2 % SIDE, wide % 2
    for ref, side in ((own, core), (twin, 1 - core)):
        for outer in range(SIDE):
            for inner in range(SIDE):
                dx = jnp.where(side == 0, reach(inner), reach(outer))
                dy = jnp.where(side == 0, reach(outer), reach(inner))
                place = (y + dy + SIDE) % SIDE * 8 + (x + dx + SIDE) % SIDE * 2 + side
                block = (outer * SIDE + inner) * ROWS
                amplitudes[pl.ds(pl.multiple_of(place * ROWS, ROWS), ROWS), :] = ref[
                    block:block + ROWS, :
                ]
    span = E_LOCAL * PITCH
    for index, step in enumerate(late_steps):
        late_ref[:, index * span:(index + 1) * span] = columns_of(amplitudes, step)
    for index, step in enumerate(steps):
        ordered[:, index * span:(index + 1) * span] = columns_of(amplitudes, step)
    fill(panel, strips)
    sum_ref[...] = other[...].astype(jnp.float32) + jnp.dot(
        ordered[...], panel[...], preferred_element_type=jnp.float32
    )


def contract_late(
    irrep_s, energy_s, occ_irrep_s, occ_energy_s, tiles_a_s,
    irrep_ref, energy_ref, occ_irrep_ref, occ_energy_ref, sum_ref, late, *refs,
):
    strips, (out_hbm, panel, out, left) = refs[:-4], refs[-4:]
    wide, narrow = lax.axis_index("wide"), lax.axis_index("narrow")
    fill(panel, strips)
    a = tiles_a_s[wide // TILE] * TILE + wide % TILE
    col_sym = irrep_ref[...].reshape(1, NVIR) ^ irrep_s[a]
    col_energy = energy_s[a] + energy_ref[...].reshape(1, NVIR)
    j_sym = as_column(occ_irrep_ref[...].reshape(1, NOCC))
    j_energy = as_column(occ_energy_ref[...].reshape(1, NOCC))
    i_count = out.shape[0] // NOCC
    out[...] = jnp.dot(late[...], panel[...], preferred_element_type=jnp.float32)
    copies = []
    for local in range(i_count):
        i = narrow * i_count + local
        rows = slice(local * NOCC, (local + 1) * NOCC)
        summed = out[rows, :] + sum_ref[rows, :]
        denom = (occ_energy_s[i] + j_energy) - col_energy
        same = (j_sym ^ occ_irrep_s[i]) == col_sym
        out[rows, :] = jnp.where(same, summed / denom, 0.0)
        copies.append(
            pltpu.make_async_copy(out.at[rows, :], out_hbm.at[rows, :], left.at[local])
        )
        copies[-1].start()
    for copy in copies:
        copy.wait()


def along_ring():
    pairs = []
    for wide in range(32):
        for n in range(RING):
            to = (n + (1 if wide % 2 == 0 else -1)) % RING
            pairs.append((wide * RING + n, wide * RING + to))
    return pairs


def plane(along_x, along_y):
    pairs = []
    for i in range(32):
        y, x, core = i // 8, i // 2 % SIDE, i % 2
        dx, dy = (along_x, along_y) if core == 0 else (along_y, along_x)
        pairs.append((i, (y + dy) % SIDE * 8 + (x + dx) % SIDE * 2 + core))
    return pairs


def hop(part):
    return lax.ppermute(part, ("wide", "narrow"), along_ring())


def swap(part):
    return lax.ppermute(part, "wide", [(i, i ^ 1) for i in range(32)])


def spread(block, steps, after=()):
    return stack([block] + [lax.ppermute(block, "wide", pairs) for pairs in steps], after)


def one_pass(
    base, amplitudes, integrals, other_terms,
    occ_energy, virt_energy, occ_irrep, virt_irrep, tiles_e, tiles_a,
):
    span = E_LOCAL * PITCH
    height = other_terms.shape[0]
    mine, picks, most = pl.pallas_call(
        pack_integrals,
        out_shape=(
            jax.ShapeDtypeStruct((E_LOCAL * CAP, NVIR), integrals.dtype),
            jax.ShapeDtypeStruct((PITCH, NVIR), jnp.bfloat16),
            jax.ShapeDtypeStruct((1,), jnp.int32),
        ),
        in_specs=[SMEM] * 4 + [VMEM, ANY],
        out_specs=(VMEM, VMEM, SMEM),
        scratch_shapes=[
            pltpu.VMEM((E_LOCAL, NVIR, NVIR), integrals.dtype),
            pltpu.SemaphoreType.DMA((E_LOCAL,)),
        ],
        compiler_params=params(8),
        name="pack_integrals",
    )(base, virt_irrep, tiles_e, tiles_a, virt_irrep, integrals)
    block = pl.pallas_call(
        pack_amplitudes,
        out_shape=jax.ShapeDtypeStruct((ROWS, TILE * PITCH), amplitudes.dtype),
        in_specs=[SMEM] * 3 + [VMEM] * 3,
        out_specs=VMEM,
        scratch_shapes=[pltpu.VMEM((TILE * ROWS, NVIR), amplitudes.dtype)],
        compiler_params=params(6),
        name="pack_amplitudes",
    )(virt_irrep, occ_irrep, tiles_e, virt_irrep, picks, amplitudes)

    strips = [mine]
    twins = swap(mine)
    rounds = []
    for _ in range(RING // 2 - 1):
        mine, twins = hop(mine), hop(twins)
        rounds.append((mine, twins))
        strips += [mine, swap(twins)]
    strips.append(hop(mine))

    own = spread(block, [plane(1, 0), plane(-1, 0), plane(2, 0)], rounds[0])
    own = spread(own, [plane(0, 1), plane(0, -1), plane(0, 2)], rounds[1])
    twin = swap(own)

    steps = [0] + [sign * r for r in range(1, RING // 2) for sign in (1, -1)] + [RING // 2]
    early = 5
    sums, late = pl.pallas_call(
        lambda *refs: contract_early(steps[:early], steps[early:], *refs),
        out_shape=(
            jax.ShapeDtypeStruct(other_terms.shape, jnp.float32),
            jax.ShapeDtypeStruct((height, (RING - early) * span), amplitudes.dtype),
        ),
        in_specs=[VMEM] * (3 + early),
        out_specs=(VMEM, VMEM),
        scratch_shapes=[
            pltpu.VMEM((height, RING * span), amplitudes.dtype),
            pltpu.VMEM((height, early * span), amplitudes.dtype),
            pltpu.VMEM((early * span, NVIR), integrals.dtype),
        ],
        compiler_params=params(20),
        name="contract_early",
    )(other_terms, own, twin, *strips[:early])
    updated = pl.pallas_call(
        contract_late,
        out_shape=jax.ShapeDtypeStruct(other_terms.shape, jnp.float32),
        in_specs=[SMEM] * 5 + [VMEM] * (6 + RING - early),
        out_specs=HBM,
        scratch_shapes=[
            pltpu.VMEM(((RING - early) * span, NVIR), integrals.dtype),
            pltpu.VMEM(other_terms.shape, jnp.float32),
            pltpu.SemaphoreType.DMA((height // NOCC,)),
        ],
        compiler_params=params(16),
        name="contract_late",
    )(
        virt_irrep, virt_energy, occ_irrep, occ_energy, tiles_a,
        virt_irrep, virt_energy, occ_irrep, occ_energy, sums, late, *strips[early:],
    )
    return updated, most[0]


def shards(amplitudes, integrals, other_terms, *tables):
    def more(state):
        return state[0] < state[2]

    def add_pass(state):
        base, total, most = state
        part, _ = one_pass(
            base.reshape(1), amplitudes, integrals, jnp.zeros_like(other_terms), *tables
        )
        return base + CAP, total + part, most

    whole, most = one_pass(
        jnp.zeros((1,), jnp.int32), amplitudes, integrals, other_terms, *tables
    )
    return lax.while_loop(more, add_pass, (jnp.int32(CAP), whole, most))[1]


def solution(mesh):
    in_specs = (
        P(("narrow", "wide"), None),
        P("narrow", "wide"),
        P("narrow", "wide"),
        P(),
        P(),
        P(),
        P(),
        P(),
        P(),
    )
    out_specs = P("narrow", "wide")
    return jax.shard_map(shards, mesh=mesh, in_specs=in_specs, out_specs=out_specs, check_vma=False)
```

```python
import functools

import jax
import jax.numpy as jnp
from jax import lax
from jax.experimental import pallas as pl
from jax.experimental.pallas import tpu as pltpu
from jax.sharding import PartitionSpec as P

TILE = 16
NVIR = 640
NOCC = 64
IRREPS = 8
CAP = 112
PITCH = 128
E_LOCAL = 2
RING = 8
SIDE = 4
ROWS = 16

SMEM = pl.BlockSpec(memory_space=pltpu.SMEM)
VMEM = pl.BlockSpec(memory_space=pltpu.VMEM)
ANY = pl.BlockSpec(memory_space=pl.ANY)
HBM = pl.BlockSpec(memory_space=pltpu.HBM)


def params(mib):
    return pltpu.CompilerParams(vmem_limit_bytes=mib * 1024 * 1024)


def pack_integrals(
    base_s, irrep_s, tiles_e_s, tiles_a_s, irrep_ref, panel_hbm,
    strip_ref, picks_ref, most_s, panel_ref, arrived,
):
    fetches = [
        pltpu.make_async_copy(
            panel_hbm.at[pl.ds(local * NVIR, NVIR), :], panel_ref.at[local], arrived.at[local]
        )
        for local in range(E_LOCAL)
    ]
    for fetch in fetches:
        fetch.start()
    wide, narrow = lax.axis_index("wide"), lax.axis_index("narrow")
    irreps = irrep_ref[...].reshape(1, NVIR)
    group = lax.broadcasted_iota(jnp.int32, (IRREPS, NVIR), 0)
    member = irreps == group
    earlier = lax.broadcasted_iota(jnp.int32, (NVIR, NVIR), 0) < lax.broadcasted_iota(
        jnp.int32, (NVIR, NVIR), 1
    )
    before = jnp.dot(
        member.astype(jnp.bfloat16),
        earlier.astype(jnp.bfloat16),
        preferred_element_type=jnp.float32,
    )
    rank = jnp.sum(jnp.where(member, before, 0.0), axis=0, keepdims=True).astype(jnp.int32)
    slots = lax.broadcasted_iota(jnp.int32, (PITCH, NVIR), 0)
    picks = ((slots == rank - base_s[0]) & (slots < CAP)).astype(jnp.bfloat16)
    picks_ref[...] = picks

    a = tiles_a_s[wide // TILE] * TILE + wide % TILE
    labels = jnp.broadcast_to(irreps, (PITCH, NVIR)).astype(jnp.float32)
    label_col = jnp.transpose(labels).astype(jnp.bfloat16)
    for local in range(E_LOCAL):
        e = tiles_e_s[0] * TILE + narrow * E_LOCAL + local
        wanted = (irreps ^ (irrep_s[a] ^ irrep_s[e])).astype(jnp.float32).astype(jnp.bfloat16)
        fetches[local].wait()
        for start in range(0, NVIR, 2 * PITCH):
            kept = []
            for tile in range(start, min(start + 2 * PITCH, NVIR), PITCH):
                lanes = slice(tile, tile + PITCH)
                held = panel_ref[local, :, lanes]
                kept.append(jnp.where(label_col == wanted[:, lanes], held, jnp.zeros_like(held)))
            kept = jnp.concatenate(kept, axis=1)
            strip_ref[local * CAP:(local + 1) * CAP, start:start + kept.shape[1]] = jnp.dot(
                picks[:CAP, :], kept, preferred_element_type=jnp.float32
            ).astype(strip_ref.dtype)
    most_s[0] = jnp.max(rank) + 1


def pack_amplitudes(irrep_s, occ_s, tiles_e_s, irrep_ref, picks_ref, rows_ref, out_ref, stacked):
    wide, narrow = lax.axis_index("wide"), lax.axis_index("narrow")
    irreps = irrep_ref[...].reshape(1, NVIR)
    first = (narrow * 32 + wide) * ROWS
    line = lax.broadcasted_iota(jnp.int32, (ROWS, NVIR), 0)
    occ = jnp.zeros((ROWS, NVIR), jnp.int32)
    for row in range(ROWS):
        pair = first + row
        occ = jnp.where(line == row, occ_s[pair // NOCC] ^ occ_s[pair % NOCC], occ)
    kin = (occ ^ irreps).astype(jnp.float32).astype(jnp.bfloat16)
    for e in range(TILE):
        held = rows_ref[:, e * NVIR:(e + 1) * NVIR]
        label = irrep_s[tiles_e_s[0] * TILE + e].astype(jnp.float32).astype(jnp.bfloat16)
        stacked[e * ROWS:(e + 1) * ROWS, :] = jnp.where(kin == label, held, jnp.zeros_like(held))
    picked = lax.dot_general(
        stacked[...], picks_ref[...], (((1,), (1,)), ((), ())), preferred_element_type=jnp.float32
    ).astype(out_ref.dtype)
    for e in range(TILE):
        out_ref[:, e * PITCH:(e + 1) * PITCH] = picked[e * ROWS:(e + 1) * ROWS, :]


def stack(parts, after=()):
    height, width = parts[0].shape

    def place(*refs):
        for index in range(len(parts)):
            refs[-1][index * height:(index + 1) * height, :] = refs[index][...]

    return pl.pallas_call(
        place,
        out_shape=jax.ShapeDtypeStruct((len(parts) * height, width), parts[0].dtype),
        in_specs=[VMEM] * len(parts) + [ANY] * len(after),
        out_specs=VMEM,
        compiler_params=params(6),
        name="stack",
    )(*parts, *after)


def as_column(row):
    width = row.shape[1]
    across = lax.broadcasted_iota(jnp.int32, (width, width), 1)
    down = lax.broadcasted_iota(jnp.int32, (width, width), 0)
    return jnp.sum(jnp.where(across == down, row, jnp.zeros_like(row)), axis=1, keepdims=True)


def reach(index):
    return (0, -1, 1, 2)[index]


def fill(panel, strips):
    blank = jnp.zeros((PITCH - CAP, NVIR), panel.dtype)
    for index, strip in enumerate(strips):
        for local in range(E_LOCAL):
            start = (index * E_LOCAL + local) * PITCH
            panel[start:start + CAP, :] = strip[local * CAP:(local + 1) * CAP, :]
            panel[start + CAP:start + PITCH, :] = blank


def place_rows(steps, split, groups, ordered, late_ref):
    wide, narrow = lax.axis_index("wide"), lax.axis_index("narrow")
    y, x, core = wide // 8, wide // 2 % SIDE, wide % 2
    way = 1 - 2 * core
    span = E_LOCAL * PITCH
    starts = [
        pl.multiple_of((narrow - way * step + RING) % RING * span, span) for step in steps
    ]
    for piece, outer, twin in groups:
        side = 1 - core if twin else core
        for inner in range(SIDE):
            dx = jnp.where(side == 0, reach(inner), reach(outer))
            dy = jnp.where(side == 0, reach(outer), reach(inner))
            place = (y + dy + SIDE) % SIDE * 8 + (x + dx + SIDE) % SIDE * 2 + side
            to_rows = pl.ds(pl.multiple_of(place * ROWS, ROWS), ROWS)
            block = slice(inner * ROWS, (inner + 1) * ROWS)
            for k, start in enumerate(starts):
                target, at = (ordered, k) if k < split else (late_ref, k - split)
                target[to_rows, at * span:(at + 1) * span] = piece[block, pl.ds(start, span)]


def contract_early(
    steps, split,
    irrep_s, energy_s, occ_irrep_s, occ_energy_s, tiles_a_s,
    irrep_ref, energy_ref, occ_irrep_ref, occ_energy_ref, other_hbm, *refs,
):
    pieces_hbm, strips = refs[:2 * SIDE], refs[2 * SIDE:-7]
    sum_ref, scale_ref, late_ref, other, ordered, panel, arrived = refs[-7:]
    fetches = [pltpu.make_async_copy(other_hbm, other, arrived.at[0])]
    for fetch in fetches:
        fetch.start()
    fill(panel, strips)
    wide, narrow = lax.axis_index("wide"), lax.axis_index("narrow")
    a = tiles_a_s[wide // TILE] * TILE + wide % TILE
    col_sym = irrep_ref[...].reshape(1, NVIR) ^ irrep_s[a]
    col_energy = energy_s[a] + energy_ref[...].reshape(1, NVIR)
    j_sym = as_column(occ_irrep_ref[...].reshape(1, NOCC))
    j_energy = as_column(occ_energy_ref[...].reshape(1, NOCC))
    i_count = scale_ref.shape[0] // NOCC
    for local in range(i_count):
        i = narrow * i_count + local
        denom = (occ_energy_s[i] + j_energy) - col_energy
        same = (j_sym ^ occ_irrep_s[i]) == col_sym
        scale_ref[local * NOCC:(local + 1) * NOCC, :] = jnp.where(same, 1.0 / denom, 0.0)
    for fetch in fetches:
        fetch.wait()
    groups = [(pieces_hbm[index], index % SIDE, index >= SIDE) for index in range(2 * SIDE)]
    place_rows(steps, split, groups, ordered, late_ref)
    sum_ref[...] = other[...].astype(jnp.float32) + jnp.dot(
        ordered[...], panel[...], preferred_element_type=jnp.float32
    )


def contract_late(sum_ref, scale_ref, late, *refs):
    strips, (out_hbm, panel, out, left) = refs[:-4], refs[-4:]
    fill(panel, strips)
    out[...] = jnp.dot(late[...], panel[...], preferred_element_type=jnp.float32)
    count = left.shape[0]
    height = out.shape[0] // count
    copies = []
    for index in range(count):
        rows = slice(index * height, (index + 1) * height)
        out[rows, :] = (out[rows, :] + sum_ref[rows, :]) * scale_ref[rows, :]
        copies.append(
            pltpu.make_async_copy(out.at[rows, :], out_hbm.at[rows, :], left.at[index])
        )
        copies[-1].start()
    for copy in copies:
        copy.wait()


def along_ring():
    pairs = []
    for wide in range(32):
        for n in range(RING):
            to = (n + (1 if wide % 2 == 0 else -1)) % RING
            pairs.append((wide * RING + n, wide * RING + to))
    return pairs


def plane(along_x, along_y):
    pairs = []
    for i in range(32):
        y, x, core = i // 8, i // 2 % SIDE, i % 2
        dx, dy = (along_x, along_y) if core == 0 else (along_y, along_x)
        pairs.append((i, (y + dy) % SIDE * 8 + (x + dx) % SIDE * 2 + core))
    return pairs


def hop(part):
    return lax.ppermute(part, ("wide", "narrow"), along_ring())


def swap(part):
    return lax.ppermute(part, "wide", [(i, i ^ 1) for i in range(32)])


def to(part, pairs):
    return lax.ppermute(part, "wide", pairs)


def one_pass(
    base, amplitudes, integrals, other_terms,
    occ_energy, virt_energy, occ_irrep, virt_irrep, tiles_e, tiles_a,
):
    span = E_LOCAL * PITCH
    height = other_terms.shape[0]
    mine, picks, most = pl.pallas_call(
        pack_integrals,
        out_shape=(
            jax.ShapeDtypeStruct((E_LOCAL * CAP, NVIR), integrals.dtype),
            jax.ShapeDtypeStruct((PITCH, NVIR), jnp.bfloat16),
            jax.ShapeDtypeStruct((1,), jnp.int32),
        ),
        in_specs=[SMEM] * 4 + [VMEM, ANY],
        out_specs=(VMEM, VMEM, SMEM),
        scratch_shapes=[
            pltpu.VMEM((E_LOCAL, NVIR, NVIR), integrals.dtype),
            pltpu.SemaphoreType.DMA((E_LOCAL,)),
        ],
        compiler_params=params(8),
        name="pack_integrals",
    )(base, virt_irrep, tiles_e, tiles_a, virt_irrep, integrals)
    block = pl.pallas_call(
        pack_amplitudes,
        out_shape=jax.ShapeDtypeStruct((ROWS, TILE * PITCH), amplitudes.dtype),
        in_specs=[SMEM] * 3 + [VMEM] * 3,
        out_specs=VMEM,
        scratch_shapes=[pltpu.VMEM((TILE * ROWS, NVIR), amplitudes.dtype)],
        compiler_params=params(6),
        name="pack_amplitudes",
    )(virt_irrep, occ_irrep, tiles_e, virt_irrep, picks, amplitudes)

    ready = lax.optimization_barrier
    mine0, twins0 = mine, swap(mine)
    mine1, twins1 = hop(mine0), hop(twins0)
    line = stack(
        [block] + [to(block, plane(*step)) for step in ((1, 0), (-1, 0), (2, 0))],
        [mine1, twins1],
    )
    line, twins1 = ready((line, twins1))
    mine2, twins2 = hop(mine1), hop(twins1)
    mine3, twins3 = hop(mine2), hop(twins2)
    pieces = [line] + [to(line, plane(0, step)) for step in (1, -1, 2)]
    pieces += [swap(piece) for piece in pieces]
    strips = [
        mine0, mine1, swap(twins1), mine2, swap(twins2), mine3, swap(twins3), hop(mine3)
    ]

    steps = [0, 1, -1, 2, -2, 3, -3, 4]
    early = 6
    full = jax.ShapeDtypeStruct(other_terms.shape, jnp.float32)
    sums, scale, late = pl.pallas_call(
        functools.partial(contract_early, steps, early),
        out_shape=(
            full, full, jax.ShapeDtypeStruct((height, (RING - early) * span), amplitudes.dtype)
        ),
        in_specs=[SMEM] * 5 + [VMEM] * 4 + [HBM] + [VMEM] * (2 * SIDE + early),
        out_specs=(VMEM,) * 3,
        scratch_shapes=[
            pltpu.VMEM(other_terms.shape, other_terms.dtype),
            pltpu.VMEM((height, early * span), amplitudes.dtype),
            pltpu.VMEM((early * span, NVIR), integrals.dtype),
            pltpu.SemaphoreType.DMA((2 * SIDE + 1,)),
        ],
        cost_estimate=pl.CostEstimate(
            flops=2 * height * early * span * NVIR, bytes_accessed=40 * 2**20, transcendentals=0
        ),
        compiler_params=params(8),
        name="contract_early",
    )(
        virt_irrep, virt_energy, occ_irrep, occ_energy, tiles_a,
        virt_irrep, virt_energy, occ_irrep, occ_energy, other_terms, *pieces, *strips[:early],
    )
    updated = pl.pallas_call(
        contract_late,
        out_shape=full,
        in_specs=[VMEM] * (3 + RING - early),
        out_specs=HBM,
        scratch_shapes=[
            pltpu.VMEM(((RING - early) * span, NVIR), integrals.dtype),
            pltpu.VMEM(other_terms.shape, jnp.float32),
            pltpu.SemaphoreType.DMA((4,)),
        ],
        compiler_params=params(6),
        name="contract_late",
    )(sums, scale, late, *strips[early:])
    return updated, most[0]


def shards(amplitudes, integrals, other_terms, *tables):
    def more(state):
        return state[0] < state[2]

    def add_pass(state):
        base, total, most = state
        part, _ = one_pass(
            base.reshape(1), amplitudes, integrals, jnp.zeros_like(other_terms), *tables
        )
        return base + CAP, total + part, most

    whole, most = one_pass(
        jnp.zeros((1,), jnp.int32), amplitudes, integrals, other_terms, *tables
    )
    return lax.while_loop(more, add_pass, (jnp.int32(CAP), whole, most))[1]


def solution(mesh):
    in_specs = (
        P(("narrow", "wide"), None),
        P("narrow", "wide"),
        P("narrow", "wide"),
        P(),
        P(),
        P(),
        P(),
        P(),
        P(),
    )
    out_specs = P("narrow", "wide")
    return jax.shard_map(shards, mesh=mesh, in_specs=in_specs, out_specs=out_specs, check_vma=False)
```

```python
import functools

import jax
import jax.numpy as jnp
from jax import lax
from jax.experimental import pallas as pl
from jax.experimental.pallas import tpu as pltpu
from jax.sharding import PartitionSpec as P

TILE = 16
NVIR = 640
NOCC = 64
IRREPS = 8
CAP = 112
PITCH = 128
E_LOCAL = 2
RING = 8
SIDE = 4
ROWS = 16

SMEM = pl.BlockSpec(memory_space=pltpu.SMEM)
VMEM = pl.BlockSpec(memory_space=pltpu.VMEM)
ANY = pl.BlockSpec(memory_space=pl.ANY)
HBM = pl.BlockSpec(memory_space=pltpu.HBM)


def params(mib):
    return pltpu.CompilerParams(vmem_limit_bytes=mib * 1024 * 1024)


def ranks(irreps):
    tiles = [irreps[:, tile:tile + PITCH] for tile in range(0, NVIR, PITCH)]
    group = lax.broadcasted_iota(jnp.int32, (IRREPS, PITCH), 0)
    members = [jnp.where(tile == group, 1.0, 0.0) for tile in tiles]
    earlier = lax.broadcasted_iota(jnp.int32, (PITCH, PITCH), 0) < lax.broadcasted_iota(
        jnp.int32, (PITCH, PITCH), 1
    )
    inside = jnp.dot(
        jnp.concatenate(members, axis=0).astype(jnp.bfloat16),
        earlier.astype(jnp.bfloat16),
        preferred_element_type=jnp.float32,
    )
    found = []
    so_far = jnp.zeros((IRREPS, 1), jnp.float32)
    for index, member in enumerate(members):
        before = inside[index * IRREPS:(index + 1) * IRREPS, :] + so_far
        found.append(jnp.sum(member * before, axis=0, keepdims=True))
        so_far = so_far + jnp.sum(member, axis=1, keepdims=True)
    return jnp.concatenate(found, axis=1).astype(jnp.int32)


def pack_integrals(
    base_s, irrep_s, tiles_e_s, tiles_a_s, irrep_ref, panel_hbm,
    strip_ref, picks_ref, most_s, panel_ref, arrived,
):
    fetches = [
        pltpu.make_async_copy(
            panel_hbm.at[pl.ds(local * NVIR, NVIR), :], panel_ref.at[local], arrived.at[local]
        )
        for local in range(E_LOCAL)
    ]
    for fetch in fetches:
        fetch.start()
    wide, narrow = lax.axis_index("wide"), lax.axis_index("narrow")
    irreps = irrep_ref[...].reshape(1, NVIR)
    rank = ranks(irreps)
    slots = lax.broadcasted_iota(jnp.int32, (PITCH, NVIR), 0)
    picks = ((slots == rank - base_s[0]) & (slots < CAP)).astype(jnp.bfloat16)
    picks_ref[...] = picks

    a = tiles_a_s[wide // TILE] * TILE + wide % TILE
    labels = jnp.broadcast_to(irreps, (PITCH, NVIR)).astype(jnp.float32)
    label_col = jnp.transpose(labels).astype(jnp.bfloat16)
    for local in range(E_LOCAL):
        e = tiles_e_s[0] * TILE + narrow * E_LOCAL + local
        wanted = (irreps ^ (irrep_s[a] ^ irrep_s[e])).astype(jnp.float32).astype(jnp.bfloat16)
        fetches[local].wait()
        for start in range(0, NVIR, 2 * PITCH):
            kept = []
            for tile in range(start, min(start + 2 * PITCH, NVIR), PITCH):
                lanes = slice(tile, tile + PITCH)
                held = panel_ref[local, :, lanes]
                kept.append(jnp.where(label_col == wanted[:, lanes], held, jnp.zeros_like(held)))
            kept = jnp.concatenate(kept, axis=1)
            strip_ref[local * CAP:(local + 1) * CAP, start:start + kept.shape[1]] = jnp.dot(
                picks[:CAP, :], kept, preferred_element_type=jnp.float32
            ).astype(strip_ref.dtype)
    most_s[0] = jnp.max(rank) + 1


def pack_amplitudes(irrep_s, occ_s, tiles_e_s, irrep_ref, picks_ref, rows_ref, out_ref, stacked):
    wide, narrow = lax.axis_index("wide"), lax.axis_index("narrow")
    irreps = irrep_ref[...].reshape(1, NVIR)
    first = (narrow * 32 + wide) * ROWS
    line = lax.broadcasted_iota(jnp.int32, (ROWS, NVIR), 0)
    occ = jnp.zeros((ROWS, NVIR), jnp.int32)
    for row in range(ROWS):
        pair = first + row
        occ = jnp.where(line == row, occ_s[pair // NOCC] ^ occ_s[pair % NOCC], occ)
    kin = (occ ^ irreps).astype(jnp.float32).astype(jnp.bfloat16)
    for e in range(TILE):
        held = rows_ref[:, e * NVIR:(e + 1) * NVIR]
        label = irrep_s[tiles_e_s[0] * TILE + e].astype(jnp.float32).astype(jnp.bfloat16)
        stacked[e * ROWS:(e + 1) * ROWS, :] = jnp.where(kin == label, held, jnp.zeros_like(held))
    picked = lax.dot_general(
        stacked[...], picks_ref[...], (((1,), (1,)), ((), ())), preferred_element_type=jnp.float32
    ).astype(out_ref.dtype)
    for e in range(TILE):
        out_ref[:, e * PITCH:(e + 1) * PITCH] = picked[e * ROWS:(e + 1) * ROWS, :]


def stack(parts, after=()):
    height, width = parts[0].shape

    def place(*refs):
        for index in range(len(parts)):
            refs[-1][index * height:(index + 1) * height, :] = refs[index][...]

    return pl.pallas_call(
        place,
        out_shape=jax.ShapeDtypeStruct((len(parts) * height, width), parts[0].dtype),
        in_specs=[VMEM] * len(parts) + [ANY] * len(after),
        out_specs=VMEM,
        compiler_params=params(6),
        name="stack",
    )(*parts, *after)


def as_column(row):
    width = row.shape[1]
    across = lax.broadcasted_iota(jnp.int32, (width, width), 1)
    down = lax.broadcasted_iota(jnp.int32, (width, width), 0)
    return jnp.sum(jnp.where(across == down, row, jnp.zeros_like(row)), axis=1, keepdims=True)


def reach(index):
    return (0, -1, 1, 2)[index]


def fill(panel, strips):
    blank = jnp.zeros((PITCH - CAP, NVIR), panel.dtype)
    for index, strip in enumerate(strips):
        for local in range(E_LOCAL):
            start = (index * E_LOCAL + local) * PITCH
            panel[start:start + CAP, :] = strip[local * CAP:(local + 1) * CAP, :]
            panel[start + CAP:start + PITCH, :] = blank


def place_rows(steps, split, groups, ordered, late_ref):
    wide, narrow = lax.axis_index("wide"), lax.axis_index("narrow")
    y, x, core = wide // 8, wide // 2 % SIDE, wide % 2
    way = 1 - 2 * core
    span = E_LOCAL * PITCH
    starts = [
        pl.multiple_of((narrow - way * step + RING) % RING * span, span) for step in steps
    ]
    for piece, outer, twin in groups:
        side = 1 - core if twin else core
        for inner in range(SIDE):
            dx = jnp.where(side == 0, reach(inner), reach(outer))
            dy = jnp.where(side == 0, reach(outer), reach(inner))
            place = (y + dy + SIDE) % SIDE * 8 + (x + dx + SIDE) % SIDE * 2 + side
            to_rows = pl.ds(pl.multiple_of(place * ROWS, ROWS), ROWS)
            block = slice(inner * ROWS, (inner + 1) * ROWS)
            for k, start in enumerate(starts):
                target, at = (ordered, k) if k < split else (late_ref, k - split)
                target[to_rows, at * span:(at + 1) * span] = piece[block, pl.ds(start, span)]


def contract_early(
    steps, split,
    irrep_s, energy_s, occ_irrep_s, occ_energy_s, tiles_a_s,
    irrep_ref, energy_ref, occ_irrep_ref, occ_energy_ref, other, *refs,
):
    pieces_hbm, strips = refs[:2 * SIDE], refs[2 * SIDE:-5]
    sum_ref, scale_ref, late_ref, ordered, panel = refs[-5:]
    fill(panel, strips)
    wide, narrow = lax.axis_index("wide"), lax.axis_index("narrow")
    a = tiles_a_s[wide // TILE] * TILE + wide % TILE
    col_sym = irrep_ref[...].reshape(1, NVIR) ^ irrep_s[a]
    col_energy = energy_s[a] + energy_ref[...].reshape(1, NVIR)
    j_sym = as_column(occ_irrep_ref[...].reshape(1, NOCC))
    j_energy = as_column(occ_energy_ref[...].reshape(1, NOCC))
    i_count = scale_ref.shape[0] // NOCC
    for local in range(i_count):
        i = narrow * i_count + local
        denom = (occ_energy_s[i] + j_energy) - col_energy
        same = (j_sym ^ occ_irrep_s[i]) == col_sym
        scale_ref[local * NOCC:(local + 1) * NOCC, :] = jnp.where(same, 1.0 / denom, 0.0)
    groups = [(pieces_hbm[index], index % SIDE, index >= SIDE) for index in range(2 * SIDE)]
    place_rows(steps, split, groups, ordered, late_ref)
    sum_ref[...] = other[...].astype(jnp.float32) + jnp.dot(
        ordered[...], panel[...], preferred_element_type=jnp.float32
    )


def contract_late(sum_ref, scale_ref, late, *refs):
    strips, (out_hbm, panel, out, left) = refs[:-4], refs[-4:]
    fill(panel, strips)
    out[...] = jnp.dot(late[...], panel[...], preferred_element_type=jnp.float32)
    count = left.shape[0]
    height = out.shape[0] // count
    copies = []
    for index in range(count):
        rows = slice(index * height, (index + 1) * height)
        out[rows, :] = (out[rows, :] + sum_ref[rows, :]) * scale_ref[rows, :]
        copies.append(
            pltpu.make_async_copy(out.at[rows, :], out_hbm.at[rows, :], left.at[index])
        )
        copies[-1].start()
    for copy in copies:
        copy.wait()


def along_ring():
    pairs = []
    for wide in range(32):
        for n in range(RING):
            to = (n + (1 if wide % 2 == 0 else -1)) % RING
            pairs.append((wide * RING + n, wide * RING + to))
    return pairs


def plane(along_x, along_y):
    pairs = []
    for i in range(32):
        y, x, core = i // 8, i // 2 % SIDE, i % 2
        dx, dy = (along_x, along_y) if core == 0 else (along_y, along_x)
        pairs.append((i, (y + dy) % SIDE * 8 + (x + dx) % SIDE * 2 + core))
    return pairs


def hop(part):
    return lax.ppermute(part, ("wide", "narrow"), along_ring())


def swap(part):
    return lax.ppermute(part, "wide", [(i, i ^ 1) for i in range(32)])


def to(part, pairs):
    return lax.ppermute(part, "wide", pairs)


def one_pass(
    base, amplitudes, integrals, other_terms,
    occ_energy, virt_energy, occ_irrep, virt_irrep, tiles_e, tiles_a,
):
    span = E_LOCAL * PITCH
    height = other_terms.shape[0]
    mine, picks, most = pl.pallas_call(
        pack_integrals,
        out_shape=(
            jax.ShapeDtypeStruct((E_LOCAL * CAP, NVIR), integrals.dtype),
            jax.ShapeDtypeStruct((PITCH, NVIR), jnp.bfloat16),
            jax.ShapeDtypeStruct((1,), jnp.int32),
        ),
        in_specs=[SMEM] * 4 + [VMEM, ANY],
        out_specs=(VMEM, VMEM, SMEM),
        scratch_shapes=[
            pltpu.VMEM((E_LOCAL, NVIR, NVIR), integrals.dtype),
            pltpu.SemaphoreType.DMA((E_LOCAL,)),
        ],
        compiler_params=params(8),
        name="pack_integrals",
    )(base, virt_irrep, tiles_e, tiles_a, virt_irrep, integrals)
    block = pl.pallas_call(
        pack_amplitudes,
        out_shape=jax.ShapeDtypeStruct((ROWS, TILE * PITCH), amplitudes.dtype),
        in_specs=[SMEM] * 3 + [VMEM] * 3,
        out_specs=VMEM,
        scratch_shapes=[pltpu.VMEM((TILE * ROWS, NVIR), amplitudes.dtype)],
        compiler_params=params(6),
        name="pack_amplitudes",
    )(virt_irrep, occ_irrep, tiles_e, virt_irrep, picks, amplitudes)

    ready = lax.optimization_barrier
    mine0, twins0 = mine, swap(mine)
    mine1, twins1 = hop(mine0), hop(twins0)
    line = stack(
        [block] + [to(block, plane(*step)) for step in ((1, 0), (-1, 0), (2, 0))],
        [mine1, twins1],
    )
    line, twins1 = ready((line, twins1))
    mine2, twins2 = hop(mine1), hop(twins1)
    mine3, twins3 = hop(mine2), hop(twins2)
    pieces = [line] + [to(line, plane(0, step)) for step in (1, -1, 2)]
    pieces += [swap(piece) for piece in pieces]
    strips = [
        mine0, mine1, swap(twins1), mine2, swap(twins2), mine3, swap(twins3), hop(mine3)
    ]

    steps = [0, 1, -1, 2, -2, 3, -3, 4]
    early = 6
    full = jax.ShapeDtypeStruct(other_terms.shape, jnp.float32)
    sums, scale, late = pl.pallas_call(
        functools.partial(contract_early, steps, early),
        out_shape=(
            full, full, jax.ShapeDtypeStruct((height, (RING - early) * span), amplitudes.dtype)
        ),
        in_specs=[SMEM] * 5 + [VMEM] * 4 + [VMEM] * (1 + 2 * SIDE + early),
        out_specs=(VMEM,) * 3,
        scratch_shapes=[
            pltpu.VMEM((height, early * span), amplitudes.dtype),
            pltpu.VMEM((early * span, NVIR), integrals.dtype),
        ],
        cost_estimate=pl.CostEstimate(
            flops=2 * height * early * span * NVIR, bytes_accessed=40 * 2**20, transcendentals=0
        ),
        compiler_params=params(8),
        name="contract_early",
    )(
        virt_irrep, virt_energy, occ_irrep, occ_energy, tiles_a,
        virt_irrep, virt_energy, occ_irrep, occ_energy, other_terms, *pieces, *strips[:early],
    )
    updated = pl.pallas_call(
        contract_late,
        out_shape=full,
        in_specs=[VMEM] * (3 + RING - early),
        out_specs=HBM,
        scratch_shapes=[
            pltpu.VMEM(((RING - early) * span, NVIR), integrals.dtype),
            pltpu.VMEM(other_terms.shape, jnp.float32),
            pltpu.SemaphoreType.DMA((4,)),
        ],
        compiler_params=params(6),
        name="contract_late",
    )(sums, scale, late, *strips[early:])
    return updated, most[0]


def shards(amplitudes, integrals, other_terms, *tables):
    def more(state):
        return state[0] < state[2]

    def add_pass(state):
        base, total, most = state
        part, _ = one_pass(
            base.reshape(1), amplitudes, integrals, jnp.zeros_like(other_terms), *tables
        )
        return base + CAP, total + part, most

    whole, most = one_pass(
        jnp.zeros((1,), jnp.int32), amplitudes, integrals, other_terms, *tables
    )
    return lax.while_loop(more, add_pass, (jnp.int32(CAP), whole, most))[1]


def solution(mesh):
    in_specs = (
        P(("narrow", "wide"), None),
        P("narrow", "wide"),
        P("narrow", "wide"),
        P(),
        P(),
        P(),
        P(),
        P(),
        P(),
    )
    out_specs = P("narrow", "wide")
    return jax.shard_map(shards, mesh=mesh, in_specs=in_specs, out_specs=out_specs, check_vma=False)
```
